256 devices in a mesh: wide: 64 (over z, x_lo, y), narrow: 4 (over x_hi, core).
Axes of the slice: x: 4 (x_hi: 2, x_lo: 2; x = x_hi * 2 + x_lo), y: 4, z: 8, core: 2. Of those that a mesh axis runs over, the one named last changes fastest.
Arguments:
- amplitudes: bfloat16 [24576, 8192], P(None, ('wide', 'narrow')), may hold values from -6 to 6
- integrals: bfloat16 [8192, 4096], P('wide', 'narrow'), may hold values from -0.0625 to 0.0625
- old_residual: float32 [24576, 4096], P('wide', 'narrow'), may hold values from -6 to 6
Outputs:
- new_residual: float32 [24576, 4096], P('wide', 'narrow')
The draws below stay inside these ranges and needn't reach their ends.
All inputs are finite; a program needn't handle non-finite values.
Results may differ from the reference program's by a relative error of at most 0.0003.
Values may be sent and summed in bfloat16 or wider, within the bound.
No kernel may reach another device: no remote copies, remote signals or barrier semaphores. Data moves between devices by JAX's collectives and lax.ppermute only.
A program may use at most 128 MiB of HBM per device.

```python
import jax
import jax.numpy as jnp
from jax import lax

PAIRS_ROW = 384
PAIRS = 24576
CDPAIRS = 8192
ABPAIRS = 4096
N_WIDE = 64


def steps_of(own_key, dims, shards, smallest, high):
    def one(axis_at, blocks):
        steps = jax.random.uniform(jax.random.fold_in(jax.random.fold_in(own_key, 6), axis_at), (blocks,), jnp.float32, smallest / len(shards), high / len(shards))
        return jnp.repeat(jnp.exp(steps), dims[axis_at] // blocks).reshape((-1,) + (1,) * (len(dims) - axis_at - 1))

    factor_of = one(*shards[0])
    for cut in shards[1:]:
        factor_of = factor_of * one(*cut)
    return factor_of


def bell_draw(own_key, dims, width, limit, shards=(), held_as=jnp.bfloat16):
    entries = width * jax.random.normal(own_key, dims, jnp.float32)
    if shards:
        entries = entries * steps_of(own_key, dims, shards, -0.22, 0.18)
    return jnp.clip(entries, -limit, limit).astype(held_as)


def setup_inputs(seed: int = 0) -> dict:
    seeds = jax.random.split(jax.random.key(seed), 4)
    return {
        "amplitudes": bell_draw(seeds[0], (PAIRS, CDPAIRS), 1.0, 6.0, ((1, 256),)),
        "integrals": bell_draw(seeds[1], (CDPAIRS, ABPAIRS), CDPAIRS ** -0.5, 0.0625, ((0, 64), (1, 4))),
        "old_residual": bell_draw(seeds[2], (PAIRS, ABPAIRS), 1.0, 6.0, ((0, 64), (1, 4)), jnp.float32),
    }


def reference(amplitudes, integrals, old_residual):
    blocks = amplitudes.reshape(N_WIDE, PAIRS_ROW, amplitudes.shape[1])

    def one_block(block):
        return jnp.dot(block, integrals, preferred_element_type=jnp.float32)

    ladder = lax.map(one_block, blocks).reshape(old_residual.shape)
    return old_residual + ladder
```

```python
import jax
import jax.numpy as jnp
from jax import lax
from jax.sharding import Mesh, PartitionSpec as P

AXES = ("z", "x_lo", "y", "x_hi", "core")
SIZES = (8, 2, 4, 2, 2)
SPLIT = 512


def swap(value, axis):
    return lax.ppermute(value, axis, [(0, 1), (1, 0)])


def gather(value, axis):
    return lax.all_gather(value, axis, axis=0)


def per_device(amplitudes, integrals, old_residual):
    x_lo = lax.axis_index("x_lo")
    place = lax.axis_index("x_hi") * 2 + lax.axis_index("core")
    cds = amplitudes.shape[1]
    rows, cols = old_residual.shape
    groups = integrals.reshape(4, cds, cols)
    sets = [lax.dynamic_index_in_dim(groups, place ^ s, 0, keepdims=False) for s in range(4)]
    panel = jnp.stack(sets)
    left, right = panel[..., :SPLIT], panel[..., SPLIT:]
    left = gather(gather(left, "y"), "z")
    right = gather(gather(right, "z"), "y")
    right = right.transpose(1, 0, 2, 3, 4)

    blocks = amplitudes.T.reshape(cds, 8, 2, 4, rows)

    def rows_of(side):
        sent = lax.dynamic_index_in_dim(blocks, side, 2, keepdims=False)
        sent = sent.transpose(1, 2, 0, 3).reshape(32, cds, rows)
        own = lax.all_to_all(sent, ("z", "y"), split_axis=0, concat_axis=0, tiled=True)
        far = swap(own, "x_hi")
        return jnp.stack([own, swap(own, "core"), far, swap(far, "core")], 1).reshape(-1, rows)

    def multiply(amps):
        halves = [
            lax.dot_general(
                amps, b.reshape(-1, b.shape[-1]), (((0,), (0,)), ((), ())),
                preferred_element_type=jnp.float32,
            )
            for b in (left, right)
        ]
        return jnp.concatenate(halves, 1)

    theirs = multiply(rows_of(1 - x_lo))
    received = swap(theirs, "x_lo")
    return old_residual + multiply(rows_of(x_lo)) + received


def solution(mesh):
    fine = Mesh(mesh.devices.reshape(SIZES), AXES)
    wide, narrow = ("z", "x_lo", "y"), ("x_hi", "core")
    placed = (P(None, wide + narrow), P(wide, narrow), P(wide, narrow))
    return jax.shard_map(
        per_device, mesh=fine, in_specs=placed, out_specs=P(wide, narrow), check_vma=False
    )
```

```python
import jax
import jax.numpy as jnp
from jax import lax
from jax.experimental import pallas as pl
from jax.experimental.pallas import tpu as pltpu
from jax.sharding import Mesh, PartitionSpec as P

AXES = ("z", "x_lo", "y", "x_hi", "core")
SIZES = (8, 2, 4, 2, 2)
NZ, NY, NS = 8, 4, 2
NEAR, FAR = (0, 1, 7, 2), (6, 3, 5, 4)
PANELS = (512, 512)
SENT = jnp.float16


def shift(value, axis, by):
    size = SIZES[AXES.index(axis)]
    return lax.ppermute(value, axis, [(i, (i + by) % size) for i in range(size)])


def across(value):
    return lax.ppermute(value, ("x_lo", "x_hi"), [(i, 3 - i) for i in range(4)])


def tie(*values):
    return lax.optimization_barrier(values)


def call(kernel, out_shape, args, place=None):
    vmem = pl.BlockSpec(memory_space=pltpu.VMEM)
    smem = pl.BlockSpec(memory_space=pltpu.SMEM)
    first = [] if place is None else [place]
    many = isinstance(out_shape, list)
    return pl.pallas_call(
        kernel,
        out_shape=out_shape,
        in_specs=[smem] * len(first) + [vmem] * len(args),
        out_specs=[vmem] * len(out_shape) if many else vmem,
        compiler_params=pltpu.CompilerParams(vmem_limit_bytes=16 * 2**20),
        cost_estimate=pl.CostEstimate(flops=1, bytes_accessed=1, transcendentals=0),
    )(*first, *args)


def cut_kernel(place, amps, out):
    rows = out.shape[-1] // 2
    for y in range(NY):
        for z in range(NZ):
            for side in range(2):
                at = (z * 2 + lax.rem(place[0] + 1 + side, 2)) * NY + y
                cols = pl.ds(pl.multiple_of(at * rows, 128), rows)
                out[y, z, :, side * rows : (side + 1) * rows] = amps[:, cols]


def pack_kernel(amps, out):
    for y in range(NY):
        for z in range(NZ):
            out[z, y] = amps[y, z]


def turn_kernel(place, amps, theirs, mine):
    rows = theirs.shape[0]
    for dz in range(NZ):
        from_z = lax.rem(place[0] - dz + NZ, NZ)
        block = [amps[from_z, lax.rem(place[1] - dy + NY, NY)] for dy in range(NY)]
        block = jnp.concatenate(block, 0)
        width = block.shape[0]
        theirs[:, dz * width : (dz + 1) * width] = block[:, :rows].T
        mine[:, dz * width : (dz + 1) * width] = block[:, rows:].T


def stack_kernel(col, *refs):
    *blocks, out = refs
    for i, block in enumerate(blocks):
        out[i] = block[:, :, col : col + out.shape[-1]]


def stack(blocks, col, width):
    sets, cds, _ = blocks[0].shape
    shape = jax.ShapeDtypeStruct((len(blocks), sets, cds, width), blocks[0].dtype)
    return call(lambda *refs: stack_kernel(col, *refs), shape, blocks)


def multiply(amps, near, far, col, width):
    rows = amps[0].shape[0]
    deep = amps[0].shape[1] // 2

    def kernel(a0, a1, *refs):
        near_refs, far_refs, outs = refs[:5], refs[5:9], refs[9:]

        def block_of(dz, dy, entry, at, size):
            if dz in FAR:
                return far_refs[dy][FAR.index(dz), entry, :, at : at + size]
            z, cols = NEAR.index(dz), slice(col + at, col + at + size)
            if dy == 2:
                half = len(NEAR) // 2
                return near_refs[2 + z // half][z % half, entry, :, cols]
            return near_refs[{0: 0, 1: 1, 3: 4}[dy]][z, entry, :, cols]

        for h, out in enumerate(outs):
            for at in range(0, width, 256):
                total = None
                for part in range(2):
                    block = jnp.concatenate(
                        [
                            block_of(part * 4 + dz, dy, h * NS + s, at, 256)
                            for s in range(NS)
                            for dz in range(4)
                            for dy in range(NY)
                        ],
                        0,
                    )
                    lhs = jnp.concatenate(
                        [a[:, part * deep : (part + 1) * deep] for a in (a0, a1)], 1
                    )
                    term = jnp.dot(lhs, block, preferred_element_type=jnp.float32)
                    total = term if total is None else total + term
                out[:, at : at + 256] = total

    shape = jax.ShapeDtypeStruct((rows, width), jnp.float32)
    return call(kernel, [shape, shape], [*amps, *near, *far])


def along_y(value):
    return shift(value, "y", 1), shift(value, "y", -1)


def beyond(up, down):
    half = up.shape[0] // 2
    return shift(up[:half], "y", 1), shift(down[half:], "y", -1)


def per_device(amplitudes, integrals, old_residual):
    z, x_lo, y, x_hi, core = (lax.axis_index(a) for a in AXES)
    cds = amplitudes.shape[1]
    rows, cols = old_residual.shape
    groups = integrals.reshape(2 * NS, cds, cols)

    def group(of_x, s):
        return lax.dynamic_index_in_dim(groups, of_x * NS + (core ^ s), 0, keepdims=True)

    away = jnp.concatenate([group(1 - x_hi, s) for s in range(NS)])
    here = [group(x_hi, s) for s in range(NS)]
    ints = jnp.concatenate(here + [shift(away, "x_hi", 1)])

    kind = amplitudes.dtype
    shape = jax.ShapeDtypeStruct((NY, NZ, cds, 2 * rows), kind)
    cut = call(cut_kernel, shape, [amplitudes.T], x_lo.reshape(1).astype(jnp.int32))
    ints, cut = tie(ints, cut)
    got = lax.all_to_all(cut, "y", split_axis=0, concat_axis=0, tiled=True)

    def along_z(amps):
        return lax.all_to_all(amps, "z", split_axis=0, concat_axis=0, tiled=True)

    ring = {0: ints}
    for step in (1, 2):
        ring[step] = shift(ring[step - 1], "z", 1)
        ring[NZ - step] = shift(ring[-(step - 1) % NZ], "z", -1)
    near = stack([ring[d] for d in NEAR], 0, cols)
    near, got, ring[2], ring[6] = tie(near, got, ring[2], ring[6])
    near_up, near_down = along_y(near)
    ring[3], ring[5] = shift(ring[2], "z", 1), shift(ring[6], "z", -1)
    ring[4] = shift(ring[3], "z", 1)
    shape = jax.ShapeDtypeStruct((NZ, NY, cds, 2 * rows), kind)
    packed = call(pack_kernel, shape, [got])
    far_z, packed = tie([ring[d] for d in FAR], packed)
    starts = [sum(PANELS[:i]) for i in range(len(PANELS))]
    own = [stack(far_z, at, width) for at, width in zip(starts, PANELS)]
    packed, own, near_up, near_down = tie(packed, own, near_up, near_down)
    amps = along_z(packed)

    near_two = beyond(near_up, near_down)
    near = [near, near_up, *near_two, near_down]
    far = [[own[0], *[shift(own[0], "y", d) for d in (1, 2, 3)]]]
    far[0][1], far[0][3], own[1] = tie(far[0][1], far[0][3], own[1])
    far.append([own[1], *[shift(own[1], "y", d) for d in (1, 2, 3)]])
    amps, near, far[0][2] = tie(amps, near, far[0][2])
    place = jnp.stack([z, y]).astype(jnp.int32)
    shape = jax.ShapeDtypeStruct((rows, NZ * NY * cds), kind)
    theirs, mine = call(turn_kernel, [shape, shape], [amps], place)
    theirs = [theirs, shift(theirs, "core", 1)]
    mine = [mine, shift(mine, "core", 1)]
    totals, at = [], 0
    for panel, width in zip(far, PANELS):
        first, second = multiply(theirs, near, panel, at, width)
        first = shift(first.astype(SENT), "x_lo", 1)
        second = across(second.astype(SENT))
        own, third = multiply(mine, near, panel, at, width)
        third = shift(third.astype(SENT), "x_hi", 1)
        total = own
        for term in (first, second, third):
            total = total + term.astype(jnp.float32)
        totals.append(total)
        at += width
    return old_residual + jnp.concatenate(totals, 1)


def solution(mesh):
    fine = Mesh(mesh.devices.reshape(SIZES), AXES)
    wide, narrow = ("z", "x_lo", "y"), ("x_hi", "core")
    placed = (P(None, wide + narrow), P(wide, narrow), P(wide, narrow))
    return jax.shard_map(
        per_device, mesh=fine, in_specs=placed, out_specs=P(wide, narrow), check_vma=False
    )
```

```python
import jax
import jax.numpy as jnp
from jax import lax
from jax.experimental import pallas as pl
from jax.experimental.pallas import tpu as pltpu
from jax.sharding import Mesh, PartitionSpec as P

AXES = ("z", "x_lo", "y", "x_hi", "core")
SIZES = (8, 2, 4, 2, 2)
NZ, NY, NS = 8, 4, 2
NEAR, FAR = (0, 1, 7, 2), (6, 3, 5, 4)
PANELS = (512, 512)
SENT = jnp.float16


def shift(value, axis, by):
    size = SIZES[AXES.index(axis)]
    return lax.ppermute(value, axis, [(i, (i + by) % size) for i in range(size)])


def across(value):
    return lax.ppermute(value, ("x_lo", "x_hi"), [(i, 3 - i) for i in range(4)])


def tie(*values):
    return lax.optimization_barrier(values)


def call(kernel, out_shape, args, place=None):
    vmem = pl.BlockSpec(memory_space=pltpu.VMEM)
    smem = pl.BlockSpec(memory_space=pltpu.SMEM)
    first = [] if place is None else [place]
    many = isinstance(out_shape, list)
    return pl.pallas_call(
        kernel,
        out_shape=out_shape,
        in_specs=[smem] * len(first) + [vmem] * len(args),
        out_specs=[vmem] * len(out_shape) if many else vmem,
        compiler_params=pltpu.CompilerParams(vmem_limit_bytes=16 * 2**20),
        cost_estimate=pl.CostEstimate(flops=1, bytes_accessed=1, transcendentals=0),
    )(*first, *args)


def cut_kernel(place, amps, out):
    rows = out.shape[-1] // 2
    for y in range(NY):
        for z in range(NZ):
            for side in range(2):
                at = (z * 2 + lax.rem(place[0] + 1 + side, 2)) * NY + y
                cols = pl.ds(pl.multiple_of(at * rows, 128), rows)
                out[y, z, :, side * rows : (side + 1) * rows] = amps[:, cols]


def pack_kernel(amps, out):
    for y in range(NY):
        for z in range(NZ):
            out[z, y] = amps[y, z]


def turn_kernel(place, amps, theirs, mine):
    rows = theirs.shape[0]
    for dz in range(NZ):
        from_z = lax.rem(place[0] - dz + NZ, NZ)
        block = [amps[from_z, lax.rem(place[1] - dy + NY, NY)] for dy in range(NY)]
        block = jnp.concatenate(block, 0)
        width = block.shape[0]
        theirs[:, dz * width : (dz + 1) * width] = block[:, :rows].T
        mine[:, dz * width : (dz + 1) * width] = block[:, rows:].T


def stack_kernel(col, *refs):
    *blocks, out = refs
    for i, block in enumerate(blocks):
        out[i] = block[:, :, col : col + out.shape[-1]]


def stack(blocks, col, width):
    sets, cds, _ = blocks[0].shape
    shape = jax.ShapeDtypeStruct((len(blocks), sets, cds, width), blocks[0].dtype)
    return call(lambda *refs: stack_kernel(col, *refs), shape, blocks)


def multiply(amps, near, far, col, width):
    rows = amps[0].shape[0]
    deep = amps[0].shape[1] // 2

    def kernel(a0, a1, *refs):
        near_refs, far_refs, outs = refs[:5], refs[5:-2], refs[-2:]

        def block_of(dz, dy, entry, at, size):
            group, order, base = (near_refs, NEAR, col) if dz in NEAR else (far_refs, FAR, 0)
            z, cols = order.index(dz), slice(base + at, base + at + size)
            if len(group) == NY:
                return group[dy][z, entry, :, cols]
            if dy == 2:
                half = len(order) // 2
                return group[2 + z // half][z % half, entry, :, cols]
            return group[{0: 0, 1: 1, 3: 4}[dy]][z, entry, :, cols]

        for h, out in enumerate(outs):
            for at in range(0, width, 256):
                total = None
                for part in range(2):
                    block = jnp.concatenate(
                        [
                            block_of(part * 4 + dz, dy, h * NS + s, at, 256)
                            for s in range(NS)
                            for dz in range(4)
                            for dy in range(NY)
                        ],
                        0,
                    )
                    lhs = jnp.concatenate(
                        [a[:, part * deep : (part + 1) * deep] for a in (a0, a1)], 1
                    )
                    term = jnp.dot(lhs, block, preferred_element_type=jnp.float32)
                    total = term if total is None else total + term
                out[:, at : at + 256] = total

    shape = jax.ShapeDtypeStruct((rows, width), jnp.float32)
    return call(kernel, [shape, shape], [*amps, *near, *far])


def along_y(value):
    return shift(value, "y", 1), shift(value, "y", -1)


def beyond(up, down):
    half = up.shape[0] // 2
    return shift(up[:half], "y", 1), shift(down[half:], "y", -1)


def per_device(amplitudes, integrals, old_residual):
    z, x_lo, y, x_hi, core = (lax.axis_index(a) for a in AXES)
    cds = amplitudes.shape[1]
    rows, cols = old_residual.shape
    groups = integrals.reshape(2 * NS, cds, cols)

    def group(of_x, s):
        return lax.dynamic_index_in_dim(groups, of_x * NS + (core ^ s), 0, keepdims=True)

    away = jnp.concatenate([group(1 - x_hi, s) for s in range(NS)])
    here = [group(x_hi, s) for s in range(NS)]
    ints = jnp.concatenate(here + [shift(away, "x_hi", 1)])

    kind = amplitudes.dtype
    shape = jax.ShapeDtypeStruct((NY, NZ, cds, 2 * rows), kind)
    cut = call(cut_kernel, shape, [amplitudes.T], x_lo.reshape(1).astype(jnp.int32))
    ints, cut = tie(ints, cut)
    got = lax.all_to_all(cut, "y", split_axis=0, concat_axis=0, tiled=True)

    def along_z(amps):
        return lax.all_to_all(amps, "z", split_axis=0, concat_axis=0, tiled=True)

    ring = {0: ints}
    for step in (1, 2):
        ring[step] = shift(ring[step - 1], "z", 1)
        ring[NZ - step] = shift(ring[-(step - 1) % NZ], "z", -1)
    near = stack([ring[d] for d in NEAR], 0, cols)
    near, got, ring[2], ring[6] = tie(near, got, ring[2], ring[6])
    near_up, near_down = along_y(near)
    ring[3], ring[5] = shift(ring[2], "z", 1), shift(ring[6], "z", -1)
    ring[4] = shift(ring[3], "z", 1)
    shape = jax.ShapeDtypeStruct((NZ, NY, cds, 2 * rows), kind)
    packed = call(pack_kernel, shape, [got])
    far_z, packed = tie([ring[d] for d in FAR], packed)
    starts = [sum(PANELS[:i]) for i in range(len(PANELS))]
    own = [stack(far_z, at, width) for at, width in zip(starts, PANELS)]
    packed, own, near_up, near_down = tie(packed, own, near_up, near_down)
    amps = along_z(packed)

    near_two = beyond(near_up, near_down)
    near = [near, near_up, *near_two, near_down]
    far = [[own[0], *[shift(own[0], "y", d) for d in (1, 2, 3)]]]
    far[0][1], far[0][3], own[1] = tie(far[0][1], far[0][3], own[1])
    ends = along_y(own[1])
    far.append([own[1], ends[0], *beyond(*ends), ends[1]])
    amps, near, far[0][2] = tie(amps, near, far[0][2])
    place = jnp.stack([z, y]).astype(jnp.int32)
    shape = jax.ShapeDtypeStruct((rows, NZ * NY * cds), kind)
    theirs, mine = call(turn_kernel, [shape, shape], [amps], place)
    theirs = [theirs, shift(theirs, "core", 1)]
    mine = [mine, shift(mine, "core", 1)]
    totals, at = [], 0
    for panel, width in zip(far, PANELS):
        first, second = multiply(theirs, near, panel, at, width)
        first = shift(first.astype(SENT), "x_lo", 1)
        second = across(second.astype(SENT))
        own, third = multiply(mine, near, panel, at, width)
        third = shift(third.astype(SENT), "x_hi", 1)
        total = own
        for term in (first, second, third):
            total = total + term.astype(jnp.float32)
        totals.append(total)
        at += width
    return old_residual + jnp.concatenate(totals, 1)


def solution(mesh):
    fine = Mesh(mesh.devices.reshape(SIZES), AXES)
    wide, narrow = ("z", "x_lo", "y"), ("x_hi", "core")
    placed = (P(None, wide + narrow), P(wide, narrow), P(wide, narrow))
    return jax.shard_map(
        per_device, mesh=fine, in_specs=placed, out_specs=P(wide, narrow), check_vma=False
    )
```

```python
import jax
import jax.numpy as jnp
from jax import lax
from jax.experimental import pallas as pl
from jax.experimental.pallas import tpu as pltpu
from jax.sharding import Mesh, PartitionSpec as P

AXES = ("z", "x_lo", "y", "x_hi", "core")
SIZES = (8, 2, 4, 2, 2)
NZ, NY, NS = 8, 4, 2
NEAR, FAR = (0, 1, 7, 2), (6, 3, 5, 4)
PANELS = (512, 512)
SENT = jnp.float16


def shift(value, axis, by):
    size = SIZES[AXES.index(axis)]
    return lax.ppermute(value, axis, [(i, (i + by) % size) for i in range(size)])


def across(value):
    return lax.ppermute(value, ("x_lo", "x_hi"), [(i, 3 - i) for i in range(4)])


def tie(*values):
    return lax.optimization_barrier(values)


def call(kernel, out_shape, args, place=None):
    vmem = pl.BlockSpec(memory_space=pltpu.VMEM)
    smem = pl.BlockSpec(memory_space=pltpu.SMEM)
    first = [] if place is None else [place]
    many = isinstance(out_shape, list)
    return pl.pallas_call(
        kernel,
        out_shape=out_shape,
        in_specs=[smem] * len(first) + [vmem] * len(args),
        out_specs=[vmem] * len(out_shape) if many else vmem,
        compiler_params=pltpu.CompilerParams(vmem_limit_bytes=16 * 2**20),
        cost_estimate=pl.CostEstimate(flops=1, bytes_accessed=1, transcendentals=0),
    )(*first, *args)


def cut_kernel(place, amps, out):
    rows = out.shape[-1] // 2
    for y in range(NY):
        for z in range(NZ):
            for side in range(2):
                at = (z * 2 + lax.rem(place[0] + 1 + side, 2)) * NY + y
                cols = pl.ds(pl.multiple_of(at * rows, 128), rows)
                out[y, z, :, side * rows : (side + 1) * rows] = amps[:, cols]


def pack_kernel(amps, out):
    for y in range(NY):
        for z in range(NZ):
            out[z, y] = amps[y, z]


def turn_kernel(place, amps, theirs, mine):
    rows = theirs.shape[0]
    for dz in range(NZ):
        from_z = lax.rem(place[0] - dz + NZ, NZ)
        block = [amps[from_z, lax.rem(place[1] - dy + NY, NY)] for dy in range(NY)]
        block = jnp.concatenate(block, 0)
        width = block.shape[0]
        theirs[:, dz * width : (dz + 1) * width] = block[:, :rows].T
        mine[:, dz * width : (dz + 1) * width] = block[:, rows:].T


def stack_kernel(col, *refs):
    *blocks, out = refs
    for i, block in enumerate(blocks):
        out[i] = block[:, :, col : col + out.shape[-1]]


def stack(blocks, col, width):
    sets, cds, _ = blocks[0].shape
    shape = jax.ShapeDtypeStruct((len(blocks), sets, cds, width), blocks[0].dtype)
    return call(lambda *refs: stack_kernel(col, *refs), shape, blocks)


def multiply(amps, near, far, col, width):
    rows = amps[0].shape[0]
    deep = amps[0].shape[1] // 2

    def kernel(a0, a1, *refs):
        near_refs, far_refs, outs = refs[:5], refs[5:-2], refs[-2:]

        def block_of(dz, dy, entry, at, size):
            group, order, base = (near_refs, NEAR, col) if dz in NEAR else (far_refs, FAR, 0)
            z, cols = order.index(dz), slice(base + at, base + at + size)
            if len(group) == NY:
                return group[dy][z, entry, :, cols]
            if dy == 2:
                half = len(order) // 2
                return group[2 + z // half][z % half, entry, :, cols]
            return group[{0: 0, 1: 1, 3: 4}[dy]][z, entry, :, cols]

        for h, out in enumerate(outs):
            for at in range(0, width, 256):
                total = None
                for part in range(2):
                    block = jnp.concatenate(
                        [
                            block_of(part * 4 + dz, dy, h * NS + s, at, 256)
                            for s in range(NS)
                            for dz in range(4)
                            for dy in range(NY)
                        ],
                        0,
                    )
                    lhs = jnp.concatenate(
                        [a[:, part * deep : (part + 1) * deep] for a in (a0, a1)], 1
                    )
                    term = jnp.dot(lhs, block, preferred_element_type=jnp.float32)
                    total = term if total is None else total + term
                out[:, at : at + 256] = total

    shape = jax.ShapeDtypeStruct((rows, width), jnp.float32)
    return call(kernel, [shape, shape], [*amps, *near, *far])


def along_y(value):
    return shift(value, "y", 1), shift(value, "y", -1)


def beyond(up, down):
    half = up.shape[0] // 2
    return shift(up[:half], "y", 1), shift(down[half:], "y", -1)


def per_device(amplitudes, integrals, old_residual):
    z, x_lo, y, x_hi, core = (lax.axis_index(a) for a in AXES)
    cds = amplitudes.shape[1]
    rows, cols = old_residual.shape
    groups = integrals.reshape(2 * NS, cds, cols)

    def group(of_x, s):
        return lax.dynamic_index_in_dim(groups, of_x * NS + (core ^ s), 0, keepdims=True)

    away = jnp.concatenate([group(1 - x_hi, s) for s in range(NS)])
    here = [group(x_hi, s) for s in range(NS)]
    ints = jnp.concatenate(here + [shift(away, "x_hi", 1)])

    kind = amplitudes.dtype
    shape = jax.ShapeDtypeStruct((NY, NZ, cds, 2 * rows), kind)
    cut = call(cut_kernel, shape, [amplitudes.T], x_lo.reshape(1).astype(jnp.int32))
    ints, cut = tie(ints, cut)
    got = lax.all_to_all(cut, "y", split_axis=0, concat_axis=0, tiled=True)

    def along_z(amps):
        return lax.all_to_all(amps, "z", split_axis=0, concat_axis=0, tiled=True)

    ring = {0: ints}
    for step in (1, 2):
        ring[step] = shift(ring[step - 1], "z", 1)
        ring[NZ - step] = shift(ring[-(step - 1) % NZ], "z", -1)
    near = stack([ring[d] for d in NEAR], 0, cols)
    near, got, ring[2], ring[6] = tie(near, got, ring[2], ring[6])
    near_up, near_down = along_y(near)
    ring[3], ring[5] = shift(ring[2], "z", 1), shift(ring[6], "z", -1)
    ring[4] = shift(ring[3], "z", 1)
    shape = jax.ShapeDtypeStruct((NZ, NY, cds, 2 * rows), kind)
    packed = call(pack_kernel, shape, [got])
    far_z, packed = tie([ring[d] for d in FAR], packed)
    starts = [sum(PANELS[:i]) for i in range(len(PANELS))]
    own = [stack(far_z, at, width) for at, width in zip(starts, PANELS)]
    packed, own, near_up, near_down = tie(packed, own, near_up, near_down)
    amps = along_z(packed)

    near_two = beyond(near_up, near_down)
    near = [near, near_up, *near_two, near_down]
    first = along_y(own[0])
    first, own[1] = tie(first, own[1])
    far = [[own[0], first[0], *beyond(*first), first[1]]]
    ends = along_y(own[1])
    far.append([own[1], ends[0], *beyond(*ends), ends[1]])
    amps, near, far[0] = tie(amps, near, far[0])
    place = jnp.stack([z, y]).astype(jnp.int32)
    shape = jax.ShapeDtypeStruct((rows, NZ * NY * cds), kind)
    theirs, mine = call(turn_kernel, [shape, shape], [amps], place)
    theirs = [theirs, shift(theirs, "core", 1)]
    mine = [mine, shift(mine, "core", 1)]
    totals, at = [], 0
    for panel, width in zip(far, PANELS):
        first, second = multiply(theirs, near, panel, at, width)
        first = shift(first.astype(SENT), "x_lo", 1)
        second = across(second.astype(SENT))
        own, third = multiply(mine, near, panel, at, width)
        third = shift(third.astype(SENT), "x_hi", 1)
        total = own
        for term in (first, second, third):
            total = total + term.astype(jnp.float32)
        totals.append(total)
        at += width
    return old_residual + jnp.concatenate(totals, 1)


def solution(mesh):
    fine = Mesh(mesh.devices.reshape(SIZES), AXES)
    wide, narrow = ("z", "x_lo", "y"), ("x_hi", "core")
    placed = (P(None, wide + narrow), P(wide, narrow), P(wide, narrow))
    return jax.shard_map(
        per_device, mesh=fine, in_specs=placed, out_specs=P(wide, narrow), check_vma=False
    )
```
